32 devices in a mesh: row: 4 (over z), col: 8 (over y, x, core).
Axes of the slice: x: 2, y: 2, z: 4, core: 2. Of those that a mesh axis runs over, the one named last changes fastest.
Arguments:
- star_pos: float32 [128, 3, 128], P(('row', 'col')), may hold values from -5 to 5
- star_vel: float32 [128, 3, 128], P(('row', 'col')), may hold values from -5 to 5
- star_acc: float32 [128, 3, 128], P(('row', 'col')), may hold values from -5 to 5
- star_jerk: float32 [128, 3, 128], P(('row', 'col')), may hold values from -5 to 5
- star_mass: float32 [128, 128], P(('row', 'col')), may hold values from 0.00012207031 to 0.0009765625
- active_index: int32 [32, 128], P(('row', 'col')), may hold values from 0 to 511, as said below
- send_block: int32 [32, 32, 4], P(('row', 'col')), may hold values from -1 to 3, as said below
- send_leaf: int32 [32, 32, 4], P(('row', 'col')), may hold values from -1 to 127
- galaxy_pos: float32 [4096, 3, 128], P(('row', 'col')), may hold values from -5 to 5
- galaxy_mass: float32 [4096, 128], P(('row', 'col')), may hold values from 0.0001 to 0.001
Outputs:
- star_pos_new: float32 [128, 3, 128], P(('row', 'col'))
- star_vel_new: float32 [128, 3, 128], P(('row', 'col'))
- galaxy_accel: float32 [4096, 3, 128], P(('row', 'col'))
The draws below stay inside these ranges and needn't reach their ends.
Inputs may be any that keep to these rules, and one draw needn't show every extreme that they name: `active_index`: the entries of one device's row are distinct. `send_block`: an entry is -1 exactly where the same entry of send_leaf is -1. Every device fills all 4 slots to itself, and one device receives 4 filled slots from every device.
All inputs are finite; a program needn't handle non-finite values.
Results may differ from the reference program's by a relative error of at most 0.0003.
Values sent between devices are 32-bit elements; how exact they have to be, the bound alone decides.
A program may use at most 64 MiB of HBM per device.

```python
import math
import jax
import jax.numpy as jnp
from jax import lax

STAR_DEV = 512
ACT_DEV = 128
LEAF_DEV = 128
SLOTS = 4
BLOCK = 128
LEAF = 128
STARS = 16384
SBLOCKS = 128
LEAVES = 4096
DEVICES = 32


def draw_active_index(key, part):
    keys = jax.random.split(jax.random.fold_in(key, 11), DEVICES)

    def one(item):
        return jax.random.permutation(item, STAR_DEV)[:ACT_DEV]
    return jax.vmap(one)(keys).astype(jnp.int32)


def route_table(key):
    base = jax.random.fold_in(key, 23)
    key_live, key_block, key_leaf, key_hot = jax.random.split(base, 4)
    shape = (DEVICES, DEVICES, SLOTS)
    source = jnp.arange(DEVICES, dtype=jnp.int32)[:, None, None]
    target = jnp.arange(DEVICES, dtype=jnp.int32)[None, :, None]
    hottest = jax.random.randint(key_hot, (), 0, DEVICES)
    live = (jax.random.randint(key_live, shape, 0, 2) == 0) | (target == source) | (target == hottest)
    blocks = jax.random.randint(key_block, shape, 0, STAR_DEV // BLOCK)
    leaves = jax.random.randint(key_leaf, shape, 0, LEAF_DEV)
    return (jnp.where(live, blocks, -1).astype(jnp.int32), jnp.where(live, leaves, -1).astype(jnp.int32))


def draw_send_block(key, part):
    return route_table(key)[0]


def draw_send_leaf(key, part):
    return route_table(key)[1]


def level_of(own_key, shape, cuts, least, largest):
    gain = 1.0
    for position, shards_of in cuts:
        draws = jax.random.uniform(jax.random.fold_in(jax.random.fold_in(own_key, 6), position), (shards_of,), jnp.float32, least / len(cuts), largest / len(cuts))
        gain = gain * jnp.repeat(jnp.exp(draws), shape[position] // shards_of).reshape((-1,) + (1,) * (len(shape) - 1 - position))
    return gain


def normal_values(rng, dims, deviation, bound, cuts=(), held_as=jnp.bfloat16):
    values = deviation * jax.random.normal(rng, dims, jnp.float32)
    if cuts:
        values = values * level_of(rng, dims, cuts, -0.22, 0.18)
    return jnp.clip(values, -bound, bound).astype(held_as)


def setup_inputs(seed: int = 0) -> dict:
    seeds = jax.random.split(jax.random.key(seed), 11)
    star_pos = normal_values(seeds[0], (SBLOCKS, 3, BLOCK), 1.0, 5.0, ((0, 32),), jnp.float32)
    star_vel = normal_values(seeds[1], (SBLOCKS, 3, BLOCK), 1.0, 5.0, ((0, 32),), jnp.float32)
    star_acc = normal_values(seeds[2], (SBLOCKS, 3, BLOCK), 1.0, 5.0, ((0, 32),), jnp.float32)
    star_jerk = normal_values(seeds[3], (SBLOCKS, 3, BLOCK), 1.0, 5.0, ((0, 32),), jnp.float32)
    star_mass = jnp.clip(jnp.exp(math.log(0.0009765625) - 2.0794415 * jax.random.uniform(seeds[4], (SBLOCKS, BLOCK), jnp.float32) ** level_of(seeds[4], (SBLOCKS, BLOCK), ((0, 32),), -0.2, 0.2)), 0.00012207031, 0.0009765625)
    active_index = draw_active_index(jax.random.fold_in(seeds[10], 71), 0)
    send_block = draw_send_block(jax.random.fold_in(seeds[10], 71), 0)
    send_leaf = draw_send_leaf(jax.random.fold_in(seeds[10], 71), 0)
    galaxy_pos = normal_values(seeds[8], (LEAVES, 3, LEAF), 1.0, 5.0, ((0, 32),), jnp.float32)
    galaxy_mass = jnp.clip(jnp.exp(math.log(0.001) - 2.3025852 * jax.random.uniform(seeds[9], (LEAVES, LEAF), jnp.float32) ** level_of(seeds[9], (LEAVES, LEAF), ((0, 32),), -0.2, 0.2)), 0.0001, 0.001)
    return dict(star_pos=star_pos, star_vel=star_vel, star_acc=star_acc, star_jerk=star_jerk, star_mass=star_mass, active_index=active_index, send_block=send_block, send_leaf=send_leaf, galaxy_pos=galaxy_pos, galaxy_mass=galaxy_mass)


step_length = 1.0
soft_star = 0.01
soft_galaxy = 0.04

def pair_block(apos, avel, rpos, rvel, rmass):
    delta = rpos[:, None, :] - apos[:, :, None]
    dvel = rvel[:, None, :] - avel[:, :, None]
    radius = lax.optimization_barrier(jnp.sum(delta * delta, 0)) + soft_star
    inverse = lax.rsqrt(radius)
    weight = rmass[None, :] * inverse * inverse * inverse
    along = lax.optimization_barrier(jnp.sum(delta * dvel, 0)) * inverse * inverse
    accel = lax.optimization_barrier(jnp.sum(delta * weight[None], -1))
    jerks = lax.optimization_barrier(jnp.sum((dvel - 3.0 * along[None] * delta) * weight[None], -1))
    return (accel, jerks)

def entry_terms(stars4, leaves4):
    count = stars4.shape[0]
    group = math.gcd(count, 16)

    def one(item):
        spos = item[0][:, :3]
        smass = item[0][:, 3]
        gpos = item[1][:, :3]
        gmass = item[1][:, 3]
        delta = gpos[:, :, None, :] - spos[:, :, :, None]
        radius = lax.optimization_barrier(jnp.sum(delta * delta, 1)) + soft_galaxy
        inverse = lax.rsqrt(radius)
        cube = inverse * inverse * inverse
        kick = lax.optimization_barrier(jnp.sum(delta * (gmass[:, None, :] * cube)[:, None], -1))
        pull = -lax.optimization_barrier(jnp.sum(delta * (smass[:, :, None] * cube)[:, None], 2))
        return (pull, kick)
    shaped = (stars4.reshape((count // group, group) + stars4.shape[1:]), leaves4.reshape((count // group, group) + leaves4.shape[1:]))
    pull, kick = lax.map(one, shaped)
    return (pull.reshape((count,) + pull.shape[2:]), kick.reshape((count,) + kick.shape[2:]))

def flatten(blocks):
    return blocks.transpose(1, 0, 2).reshape(3, -1)

def reference(star_pos, star_vel, star_acc, star_jerk, star_mass, active_index, send_block, send_leaf, galaxy_pos, galaxy_mass):
    half = 0.5 * step_length ** 2
    sixth = step_length ** 3 / 6.0
    pred_pos = star_pos + step_length * star_vel + half * star_acc + sixth * star_jerk
    pred_vel = star_vel + step_length * star_acc + half * star_jerk
    pos_flat = flatten(pred_pos)
    vel_flat = flatten(pred_vel)
    mass_flat = star_mass.reshape(-1)
    devices = active_index.shape[0]
    chosen = (active_index + jnp.arange(devices, dtype=jnp.int32)[:, None] * STAR_DEV).reshape(-1).astype(jnp.int32)
    apos = pos_flat[:, chosen]
    avel = vel_flat[:, chosen]
    total = apos.shape[1]
    size = math.gcd(total, 512)
    stars = pos_flat.shape[1]
    stretch = math.gcd(stars, 4096)
    rpos = pos_flat.reshape(3, stars // stretch, stretch).transpose(1, 0, 2)
    rvel = vel_flat.reshape(3, stars // stretch, stretch).transpose(1, 0, 2)
    rmass = mass_flat.reshape(stars // stretch, stretch)

    def active_group(item):

        def step(carry, piece):
            accel, jerks = pair_block(item[0], item[1], piece[0], piece[1], piece[2])
            return ((carry[0] + accel, carry[1] + jerks), None)
        start = (jnp.zeros((3, size), jnp.float32), jnp.zeros((3, size), jnp.float32))
        result, unused = lax.scan(step, start, (rpos, rvel, rmass))
        return result
    grouped = (apos.reshape(3, total // size, size).transpose(1, 0, 2), avel.reshape(3, total // size, size).transpose(1, 0, 2))
    acc_new, jerk_new = lax.map(active_group, grouped)
    acc_new = acc_new.transpose(1, 0, 2).reshape(3, total)
    jerk_new = jerk_new.transpose(1, 0, 2).reshape(3, total)
    start_acc = flatten(star_acc)[:, chosen]
    start_jerk = flatten(star_jerk)[:, chosen]
    start_pos = flatten(star_pos)[:, chosen]
    start_vel = flatten(star_vel)[:, chosen]
    vel_one = start_vel + (start_acc + acc_new) * (0.5 * step_length) + (start_jerk - jerk_new) * (step_length ** 2 / 12.0)
    pos_one = start_pos + (start_vel + vel_one) * (0.5 * step_length) + (start_acc - acc_new) * (step_length ** 2 / 12.0)
    nblock = STAR_DEV // BLOCK
    pos_new_flat = pos_flat.at[:, chosen].set(pos_one)
    vel_mid_flat = vel_flat.at[:, chosen].set(vel_one)
    star_pos_new = pos_new_flat.reshape(3, -1, BLOCK).transpose(1, 0, 2)
    vel_mid = vel_mid_flat.reshape(3, -1, BLOCK).transpose(1, 0, 2)
    packed_stars = jnp.concatenate([star_pos_new, star_mass[:, None, :]], 1)
    packed_gal = jnp.concatenate([galaxy_pos, galaxy_mass[:, None, :]], 1)

    def per_source(carry, source):
        table = send_block[source]
        leafs = send_leaf[source]
        live = (table >= 0).reshape(-1).astype(jnp.float32)[:, None, None]
        local_block = jnp.maximum(table, 0).reshape(-1).astype(jnp.int32)
        sidx = (source * nblock + local_block).astype(jnp.int32)
        gidx = (jnp.arange(devices, dtype=jnp.int32)[:, None] * LEAF_DEV + jnp.maximum(leafs, 0)).reshape(-1).astype(jnp.int32)
        stars4 = packed_stars[sidx] * live
        leaves4 = packed_gal[gidx] * live
        pull, kick = entry_terms(stars4, leaves4)
        carry = carry.at[gidx].add(pull)
        kicks = jnp.zeros((nblock, 3, BLOCK), jnp.float32).at[local_block].add(kick)
        return (carry, kicks)
    empty = jnp.zeros(galaxy_pos.shape, jnp.float32)
    pull_total, kicks = lax.scan(per_source, empty, jnp.arange(devices, dtype=jnp.int32))
    kick_all = kicks.reshape(star_pos.shape)
    star_vel_new = vel_mid + step_length * kick_all
    galaxy_accel = pull_total * (STARS / BLOCK)
    return (star_pos_new, star_vel_new, galaxy_accel)
```

```python
import functools

import jax
import jax.numpy as jnp
from jax import lax
from jax.experimental import pallas as pl
from jax.experimental.pallas import tpu as pltpu
from jax.sharding import PartitionSpec as P

MESH = pl.DeviceIdType.MESH
step_length = 1.0
half = 0.5 * step_length**2
sixth = step_length**3 / 6.0
twelfth = step_length**2 / 12.0
soft_star = 0.01
soft_galaxy = 0.04
F32 = jnp.float32
BF16 = jnp.bfloat16


def row_of(x):
    return lax.broadcasted_iota(jnp.int32, x.shape, 0)


def swap(x):
    return pltpu.roll(x, 4, 0)


def rounded(x):
    return x.astype(BF16).astype(F32)


def split3(x):
    high = rounded(x)
    rest = x - high
    mid = rounded(rest)
    return high, mid, rest - mid


def split2(x):
    high = rounded(x)
    return high, x - high


def predict(a, b):
    pos = a + step_length * swap(a) + half * b + sixth * swap(b)
    vel = a + step_length * swap(b) + half * b
    return jnp.where(row_of(a) < 4, pos, vel)


def stack_left(table):
    high, mid, low = split3(table)
    ones = jnp.where(row_of(table) < 3, 1.0, 0.0)
    return jnp.concatenate([high, high, high, mid, mid, low, ones, jnp.zeros_like(table)], 0)


def stack_right(table, const):
    high, mid, low = split3(table)
    ch, cm, cl = split3(const)
    row = row_of(table)
    last = jnp.where(row == 0, ch, jnp.where(row == 1, cm, jnp.where(row == 2, cl, 0.0)))
    return jnp.concatenate(
        [high, mid, low, high, mid, high, last, jnp.zeros_like(table)], 0
    ).astype(BF16)


def sum3(x):
    return jnp.sum(jnp.where(row_of(x) < 3, x, 0.0), 0, keepdims=True)


def dot(a, b):
    return lax.dot_general(a, b, (((1,), (0,)), ((), ())), preferred_element_type=F32)


def dot_t(a, b):
    return lax.dot_general(a, b, (((1,), (1,)), ((), ())), preferred_element_type=F32)


def cube_parts(x):
    high = x.astype(BF16)
    return high, (x - high.astype(F32)).astype(BF16)


def kernel(
    rows,
    cols,
    spos,
    svel,
    sacc,
    sjerk,
    smass,
    index,
    sblock,
    lists,
    gpos,
    gmass,
    out_pos,
    out_vel,
    pulls,
    lists_in,
    base_a,
    base_b,
    onehot,
    act_all,
    star_all,
    left,
    right2,
    rightd,
    weigh,
    acc_u,
    acc_q,
    part_out,
    part_in,
    leaves_out,
    leaves_in,
    pull_out,
    sleft,
    sfeat,
    fresh,
    lists_s,
    list_send,
    list_recv,
    act_send,
    act_recv,
    star_send,
    star_recv,
    leaf_send,
    leaf_recv,
    part_send,
    part_recv,
    pull_send,
    pull_recv,
    local_sem,
):
    mr = lax.axis_index("row")
    mc = lax.axis_index("col")
    count = rows * cols
    me = mr * cols + mc
    nblock, _, width = spos.shape
    slots = sblock.shape[2]
    stars = nblock * width
    nact = index.shape[1]

    def where_is(flat):
        return (flat // cols, flat % cols)

    barrier = pltpu.get_barrier_semaphore()

    def greet(off, carry):
        pl.semaphore_signal(
            barrier, inc=1, device_id=where_is((me + off) % count), device_id_type=MESH
        )
        return carry

    lax.fori_loop(1, count, greet, 0)

    base_a[...] = jnp.zeros_like(base_a)
    base_b[...] = jnp.zeros_like(base_b)
    for b in range(nblock):
        at = pl.ds(b * width, width)
        base_a[0:3, at] = spos[b]
        base_a[4:7, at] = svel[b]
        base_b[0:3, at] = sacc[b]
        base_b[4:7, at] = sjerk[b]
    ta = base_a[...]
    tb = base_b[...]
    pred = predict(ta, tb)
    base_a[...] = pred
    for b in range(nblock):
        at = pl.ds(b * width, width)
        base_a[3:4, at] = smass[b : b + 1, :]
    star_all[mr] = base_a[...]
    hot = lax.broadcasted_iota(jnp.int32, (stars, nact), 0) == index[...]
    onehot[...] = hot.astype(F32).astype(BF16)
    parts = jnp.concatenate(split3(ta) + split3(tb), 0).astype(BF16)
    got = dot(parts, onehot[...])
    sel_a = got[0:8] + got[8:16] + got[16:24]
    sel_b = got[24:32] + got[32:40] + got[40:48]
    mine = predict(sel_a, sel_b)
    row8 = row_of(mine)
    mine = jnp.where(
        row8 == 3, sum3(mine * mine), jnp.where(row8 == 7, sum3(mine * swap(mine)), mine)
    )
    act_all[mc] = mine

    pl.semaphore_wait(barrier, count - 1)

    def act_copy(peer, slot):
        return pltpu.make_async_remote_copy(
            src_ref=act_all.at[mc],
            dst_ref=act_all.at[mc],
            send_sem=act_send.at[peer],
            recv_sem=act_recv.at[slot],
            device_id=(mr, peer),
            device_id_type=MESH,
        )

    def star_copy(peer, slot):
        return pltpu.make_async_remote_copy(
            src_ref=star_all.at[mr],
            dst_ref=star_all.at[mr],
            send_sem=star_send.at[peer],
            recv_sem=star_recv.at[slot],
            device_id=(peer, mc),
            device_id_type=MESH,
        )

    def list_copy(peer, slot):
        return pltpu.make_async_remote_copy(
            src_ref=lists.at[peer],
            dst_ref=lists_in.at[me],
            send_sem=list_send.at[peer],
            recv_sem=list_recv.at[slot],
            device_id=where_is(peer),
            device_id_type=MESH,
        )

    def leaf_copy(peer, slot):
        return pltpu.make_async_remote_copy(
            src_ref=leaves_out.at[peer],
            dst_ref=leaves_in.at[me],
            send_sem=leaf_send.at[peer],
            recv_sem=leaf_recv.at[slot],
            device_id=where_is(peer),
            device_id_type=MESH,
        )

    def part_copy(peer, slot):
        return pltpu.make_async_remote_copy(
            src_ref=part_out.at[peer],
            dst_ref=part_in.at[mc],
            send_sem=part_send.at[peer],
            recv_sem=part_recv.at[slot],
            device_id=(mr, peer),
            device_id_type=MESH,
        )

    def pull_copy(peer, slot):
        return pltpu.make_async_remote_copy(
            src_ref=pull_out.at[peer],
            dst_ref=pulls.at[me],
            send_sem=pull_send.at[peer],
            recv_sem=pull_recv.at[slot],
            device_id=where_is(peer),
            device_id_type=MESH,
        )

    def each(size, here, act):
        def body(off, carry):
            act((here + off) % size)
            return carry

        lax.fori_loop(1, size, body, 0)

    each(cols, mc, lambda peer: act_copy(peer, mc).start())
    each(rows, mr, lambda peer: star_copy(peer, mr).start())
    each(count, me, lambda peer: list_copy(peer, me).start())
    lists_in[me] = lists[me]

    def prepare(r):
        table = star_all[r]
        row = row_of(table)
        body = (row != 3) & (row != 7)
        mass = table[3:4]
        right2[...] = stack_right(
            jnp.where(row < 3, -2.0 * table, jnp.where(row == 3, 1.0, 0.0)),
            sum3(table * table) + soft_star,
        )
        turned = swap(table)
        rightd[...] = stack_right(
            jnp.where(body, -turned, jnp.where(row == 7, 1.0, 0.0)), sum3(table * turned)
        )
        high, low = split2(jnp.where(body, table * mass, jnp.where(row == 3, mass, 0.0)))
        pad = jnp.zeros((weigh.shape[0] - 16, stars), F32)
        weigh[...] = jnp.concatenate([high, low, pad], 0).astype(BF16)

    def pairs(c):
        lhs = left[c]
        r2 = dot(lhs, right2[...])
        along = dot(lhs, rightd[...])
        inv = lax.rsqrt(r2)
        inv2 = inv * inv
        u = inv2 * inv
        q = u * inv2 * along
        uh, ul = cube_parts(u)
        qh, ql = cube_parts(q)
        w = weigh[...]
        acc_u[c] += dot_t(uh, w) + dot_t(ul, w)
        acc_q[c] += dot_t(qh, w) + dot_t(ql, w)

    def left_of(c):
        left[c] = stack_left(act_all[c]).T.astype(BF16)

    acc_u[...] = jnp.zeros_like(acc_u)
    acc_q[...] = jnp.zeros_like(acc_q)
    prepare(mr)
    left_of(mc)
    pairs(mc)

    def take_active(off, carry):
        c = (mc + off) % cols
        act_copy(c, c).wait_recv()
        left_of(c)
        pairs(c)
        return carry

    lax.fori_loop(1, cols, take_active, 0)

    each(count, me, lambda peer: list_copy(peer, peer).wait_recv())
    move = pltpu.make_async_copy(lists_in, lists_s, local_sem)
    move.start()
    move.wait()

    def grab(peer, ref):
        for s in range(slots):
            leaf = lists_s[peer, 0, s]
            live = leaf >= 0
            at = jnp.maximum(leaf, 0)
            keep = jnp.where(live, 1.0, 0.0)
            ref[peer, 4 * s : 4 * s + 3, :] = gpos[at] * keep
            ref[peer, 4 * s + 3 : 4 * s + 4, :] = gmass[pl.ds(at, 1), :] * keep

    grab(me, leaves_in)

    def serve(peer):
        grab(peer, leaves_out)
        leaf_copy(peer, me).start()

    each(count, me, serve)

    def take_stars(off, carry):
        r = (mr + off) % rows
        star_copy(r, r).wait_recv()
        prepare(r)

        def inner(c, carry):
            pairs(c)
            return carry

        lax.fori_loop(0, cols, inner, 0)
        return carry

    lax.fori_loop(1, rows, take_stars, 0)

    def finish(c):
        su = acc_u[c].T
        sq = acc_q[c].T
        su = su[0:8] + su[8:16]
        sq = sq[0:8] + sq[8:16]
        table = act_all[c]
        su = su - table * su[3:4]
        sq = sq - table * sq[3:4]
        return jnp.where(row8 < 4, su, su - 3.0 * swap(sq))

    def give(c):
        part_out[c] = finish(c)
        part_copy(c, mc).start()

    each(cols, mc, give)
    total = finish(mc)

    def collect(off, total):
        c = (mc + off) % cols
        part_copy(c, c).wait_recv()
        return total + part_in[c]

    total = lax.fori_loop(1, cols, collect, total)

    gap = (sel_b - total) * twelfth
    vel_one = sel_a + swap(sel_b + total) * (0.5 * step_length) + gap
    pos_one = sel_a + swap(sel_a + vel_one) * (0.5 * step_length) + gap
    new = jnp.where(row8 < 4, pos_one, vel_one)
    new = jnp.where(row8 == 3, 1.0, jnp.where(row8 == 7, 0.0, new))
    parts = jnp.concatenate(split3(new) + (jnp.zeros_like(new),), 0).astype(BF16)
    spread = dot_t(parts, onehot[...])
    spread = spread[0:8] + spread[8:16] + spread[16:24]
    fresh[...] = jnp.where(spread[3:4] > 0.5, spread, base_a[...])

    for b in range(nblock):
        at = pl.ds(b * width, width)
        table = fresh[:, at]
        mass = smass[b : b + 1, :]
        out_pos[b] = table[0:3]
        only = jnp.where(row8 < 3, table, 0.0)
        only = jnp.where(row8 == 3, sum3(only * only), only)
        sleft[b] = stack_left(only).T.astype(BF16)
        high, low = split2(jnp.where(row8 < 3, table * mass, jnp.where(row8 == 3, mass, 0.0)))
        both = jnp.concatenate([high, low], 0).astype(BF16)
        sfeat[b] = jnp.concatenate([both, both], 1)

    def entry(peer, s, kicks):
        block = sblock[0, peer, s]
        at = jnp.maximum(block, 0)
        leaf = leaves_in[peer, 4 * s : 4 * s + 4, :]
        leaf = jnp.concatenate([leaf, jnp.zeros_like(leaf)], 0)
        row = row_of(leaf)
        mass = leaf[3:4]
        feat = stack_right(
            jnp.where(row < 3, -2.0 * leaf, jnp.where(row == 3, 1.0, 0.0)),
            sum3(leaf * leaf) + soft_galaxy,
        )
        inv = lax.rsqrt(dot(sleft[at], feat))
        uh, ul = cube_parts(inv * inv * inv)
        high, low = split2(jnp.where(row < 3, leaf * mass, jnp.where(row == 3, mass, 0.0)))
        both = jnp.concatenate([high, low], 0).astype(BF16)
        kick = dot_t(both, uh) + dot_t(both, ul)
        kick = kick[0:8] + kick[8:16]
        pull = dot(sfeat[at], jnp.concatenate([uh, ul], 0))
        pull = pull[0:8] + pull[8:16]
        pull = pull - leaf * pull[3:4]
        return pull[0:3], tuple(
            k + jnp.where(block == b, kick, 0.0) for b, k in enumerate(kicks)
        )

    def entries(peer, ref, kicks):
        for s in range(slots):
            pull, kicks = entry(peer, s, kicks)
            ref[peer, 3 * s : 3 * s + 3, :] = pull
        return kicks

    def work(off, kicks):
        peer = (me + off) % count
        leaf_copy(peer, peer).wait_recv()
        kicks = entries(peer, pull_out, kicks)
        pull_copy(peer, me).start()
        return kicks

    kicks = tuple(jnp.zeros((8, width), F32) for _ in range(nblock))
    kicks = lax.fori_loop(1, count, work, kicks)
    kicks = entries(me, pulls, kicks)
    for b in range(nblock):
        table = fresh[:, pl.ds(b * width, width)]
        kick = kicks[b] - table * kicks[b][3:4]
        out_vel[b] = table[4:7] + step_length * kick[0:3]

    each(count, me, lambda peer: pull_copy(peer, peer).wait_recv())
    each(cols, mc, lambda peer: act_copy(peer, mc).wait_send())
    each(rows, mr, lambda peer: star_copy(peer, mr).wait_send())
    each(cols, mc, lambda peer: part_copy(peer, mc).wait_send())

    def drain(peer):
        list_copy(peer, me).wait_send()
        leaf_copy(peer, me).wait_send()
        pull_copy(peer, me).wait_send()

    each(count, me, drain)


def gather_kernel(scale, pulls, lists, pos, vel, out, out_pos, out_vel):
    count = pulls.shape[0]
    slots = pulls.shape[1] // 3
    out[...] = jnp.zeros_like(out)
    out_pos[...] = pos[...]
    out_vel[...] = vel[...]

    def body(source, carry):
        for s in range(slots):
            leaf = lists[source, 0, s]

            @pl.when(leaf >= 0)
            def add():
                out[leaf] += pulls[source, 3 * s : 3 * s + 3, :] * scale

        return carry

    lax.fori_loop(0, count, body, 0)


def local(
    rows,
    cols,
    star_pos,
    star_vel,
    star_acc,
    star_jerk,
    star_mass,
    active_index,
    send_block,
    send_leaf,
    galaxy_pos,
    galaxy_mass,
):
    count = rows * cols
    nblock, _, width = star_pos.shape
    stars = nblock * width
    nact = active_index.shape[1]
    slots = send_leaf.shape[2]
    depth = galaxy_pos.shape[2]
    lists = jnp.pad(send_leaf[0][:, None, :], ((0, 0), (0, 0), (0, 128 - slots)))
    vmem = pl.BlockSpec(memory_space=pltpu.VMEM)
    smem = pl.BlockSpec(memory_space=pltpu.SMEM)
    dma = pltpu.SemaphoreType.DMA
    pos, vel, pulls, arrived = pl.pallas_call(
        functools.partial(kernel, rows, cols),
        out_shape=(
            jax.ShapeDtypeStruct(star_pos.shape, F32),
            jax.ShapeDtypeStruct(star_vel.shape, F32),
            jax.ShapeDtypeStruct((count, 3 * slots, depth), F32),
            jax.ShapeDtypeStruct((count, 1, 128), jnp.int32),
        ),
        in_specs=[vmem] * 6 + [smem] + [vmem] * 3,
        out_specs=(vmem,) * 4,
        scratch_shapes=[
            pltpu.VMEM((8, stars), F32),
            pltpu.VMEM((8, stars), F32),
            pltpu.VMEM((stars, nact), BF16),
            pltpu.VMEM((cols, 8, nact), F32),
            pltpu.VMEM((rows, 8, stars), F32),
            pltpu.VMEM((cols, nact, 64), BF16),
            pltpu.VMEM((64, stars), BF16),
            pltpu.VMEM((64, stars), BF16),
            pltpu.VMEM((128, stars), BF16),
            pltpu.VMEM((cols, nact, 128), F32),
            pltpu.VMEM((cols, nact, 128), F32),
            pltpu.VMEM((cols, 8, nact), F32),
            pltpu.VMEM((cols, 8, nact), F32),
            pltpu.VMEM((count, 4 * slots, depth), F32),
            pltpu.VMEM((count, 4 * slots, depth), F32),
            pltpu.VMEM((count, 3 * slots, depth), F32),
            pltpu.VMEM((nblock, width, 64), BF16),
            pltpu.VMEM((nblock, 16, 2 * width), BF16),
            pltpu.VMEM((8, stars), F32),
            pltpu.SMEM((count, 1, 128), jnp.int32),
            dma((count,)),
            dma((count,)),
            dma((cols,)),
            dma((cols,)),
            dma((rows,)),
            dma((rows,)),
            dma((count,)),
            dma((count,)),
            dma((cols,)),
            dma((cols,)),
            dma((count,)),
            dma((count,)),
            dma(()),
        ],
        compiler_params=pltpu.CompilerParams(
            collective_id=0, has_side_effects=True, vmem_limit_bytes=48 * 1024 * 1024
        ),
    )(
        star_pos,
        star_vel,
        star_acc,
        star_jerk,
        star_mass,
        active_index,
        send_block,
        lists,
        galaxy_pos,
        galaxy_mass,
    )
    accel, pos, vel = pl.pallas_call(
        functools.partial(gather_kernel, float(nblock * count)),
        out_shape=(
            jax.ShapeDtypeStruct(galaxy_pos.shape, F32),
            jax.ShapeDtypeStruct(star_pos.shape, F32),
            jax.ShapeDtypeStruct(star_vel.shape, F32),
        ),
        in_specs=[vmem, smem, vmem, vmem],
        out_specs=(vmem,) * 3,
        compiler_params=pltpu.CompilerParams(vmem_limit_bytes=48 * 1024 * 1024),
    )(pulls, arrived, pos, vel)
    return (pos, vel, accel)


def solution(mesh):
    rows = mesh.shape["row"]
    cols = mesh.shape["col"]
    three = P(("row", "col"), None, None)
    two = P(("row", "col"), None)
    return jax.shard_map(
        functools.partial(local, rows, cols),
        mesh=mesh,
        in_specs=(three, three, three, three, two, two, three, three, three, two),
        out_specs=(three, three, three),
        check_vma=False,
    )
```

```python
import functools

import jax
import jax.numpy as jnp
from jax import lax
from jax.experimental import pallas as pl
from jax.experimental.pallas import tpu as pltpu
from jax.sharding import PartitionSpec as P

MESH = pl.DeviceIdType.MESH
step_length = 1.0
half = 0.5 * step_length**2
sixth = step_length**3 / 6.0
twelfth = step_length**2 / 12.0
soft_star = 0.01
soft_galaxy = 0.04
F32 = jnp.float32
BF16 = jnp.bfloat16


def row_of(x):
    return lax.broadcasted_iota(jnp.int32, x.shape, 0)


def swap(x):
    return pltpu.roll(x, 4, 0)


def rounded(x):
    return x.astype(BF16).astype(F32)


def split3(x):
    high = rounded(x)
    rest = x - high
    mid = rounded(rest)
    return high, mid, rest - mid


def split2(x):
    high = rounded(x)
    return high, x - high


def predict(a, b):
    pos = a + step_length * swap(a) + half * b + sixth * swap(b)
    vel = a + step_length * swap(b) + half * b
    return jnp.where(row_of(a) < 4, pos, vel)


def stack_left(table):
    high, mid, low = split3(table)
    ones = jnp.where(row_of(table) < 3, 1.0, 0.0)
    return jnp.concatenate([high, high, high, mid, mid, low, ones, jnp.zeros_like(table)], 0)


def stack_right(table, const):
    high, mid, low = split3(table)
    ch, cm, cl = split3(const)
    row = row_of(table)
    last = jnp.where(row == 0, ch, jnp.where(row == 1, cm, jnp.where(row == 2, cl, 0.0)))
    return jnp.concatenate(
        [high, mid, low, high, mid, high, last, jnp.zeros_like(table)], 0
    ).astype(BF16)


def sum3(x):
    return jnp.sum(jnp.where(row_of(x) < 3, x, 0.0), 0, keepdims=True)


def dot(a, b):
    return lax.dot_general(a, b, (((1,), (0,)), ((), ())), preferred_element_type=F32)


def dot_t(a, b):
    return lax.dot_general(a, b, (((1,), (1,)), ((), ())), preferred_element_type=F32)


def cube_parts(x):
    high = x.astype(BF16)
    return high, (x - high.astype(F32)).astype(BF16)


def kernel(
    rows,
    cols,
    spos,
    svel,
    sacc,
    sjerk,
    smass,
    index,
    sblock,
    lists,
    gpos,
    gmass,
    out_pos,
    out_vel,
    out_accel,
    base_a,
    base_b,
    onehot,
    act_all,
    star_all,
    left,
    right2,
    rightd,
    weigh,
    acc_u,
    acc_q,
    part_out,
    part_in,
    leaves_out,
    leaves_in,
    pull_out,
    pulls,
    keys,
    pick,
    kicks,
    sleft,
    sfeat,
    fresh,
    lists_in,
    lists_s,
    list_send,
    list_recv,
    act_send,
    act_recv,
    star_send,
    star_recv,
    leaf_send,
    leaf_recv,
    part_send,
    part_recv,
    pull_send,
    pull_recv,
    local_sem,
):
    mr = lax.axis_index("row")
    mc = lax.axis_index("col")
    count = rows * cols
    me = mr * cols + mc
    _, nblock, width = spos.shape
    slots = sblock.shape[0]
    stars = nblock * width
    nact = index.shape[1]

    def where_is(flat):
        return (flat // cols, flat % cols)

    barrier = pltpu.get_barrier_semaphore()

    def greet(off, carry):
        pl.semaphore_signal(
            barrier, inc=1, device_id=where_is((me + off) % count), device_id_type=MESH
        )
        return carry

    lax.fori_loop(1, count, greet, 0)

    base_a[...] = jnp.zeros_like(base_a)
    base_b[...] = jnp.zeros_like(base_b)
    for b in range(nblock):
        at = pl.ds(b * width, width)
        base_a[0:3, at] = spos[:, b, :]
        base_a[4:7, at] = svel[:, b, :]
        base_b[0:3, at] = sacc[:, b, :]
        base_b[4:7, at] = sjerk[:, b, :]
    ta = base_a[...]
    tb = base_b[...]
    pred = predict(ta, tb)
    base_a[...] = pred
    for b in range(nblock):
        at = pl.ds(b * width, width)
        base_a[3:4, at] = smass[b : b + 1, :]
    star_all[mr] = base_a[...]
    hot = lax.broadcasted_iota(jnp.int32, (stars, nact), 0) == index[...]
    onehot[...] = hot.astype(F32).astype(BF16)
    parts = jnp.concatenate(split3(ta) + split3(tb), 0).astype(BF16)
    got = dot(parts, onehot[...])
    sel_a = got[0:8] + got[8:16] + got[16:24]
    sel_b = got[24:32] + got[32:40] + got[40:48]
    mine = predict(sel_a, sel_b)
    row8 = row_of(mine)
    mine = jnp.where(
        row8 == 3, sum3(mine * mine), jnp.where(row8 == 7, sum3(mine * swap(mine)), mine)
    )
    act_all[mc] = mine

    pl.semaphore_wait(barrier, count - 1)

    def act_copy(peer, slot):
        return pltpu.make_async_remote_copy(
            src_ref=act_all.at[mc],
            dst_ref=act_all.at[mc],
            send_sem=act_send.at[peer],
            recv_sem=act_recv.at[slot],
            device_id=(mr, peer),
            device_id_type=MESH,
        )

    def star_copy(peer, slot):
        return pltpu.make_async_remote_copy(
            src_ref=star_all.at[mr],
            dst_ref=star_all.at[mr],
            send_sem=star_send.at[peer],
            recv_sem=star_recv.at[slot],
            device_id=(peer, mc),
            device_id_type=MESH,
        )

    def list_copy(peer, slot):
        return pltpu.make_async_remote_copy(
            src_ref=lists.at[peer],
            dst_ref=lists_in.at[me],
            send_sem=list_send.at[peer],
            recv_sem=list_recv.at[slot],
            device_id=where_is(peer),
            device_id_type=MESH,
        )

    def leaf_copy(peer, slot):
        return pltpu.make_async_remote_copy(
            src_ref=leaves_out.at[peer],
            dst_ref=leaves_in.at[me],
            send_sem=leaf_send.at[peer],
            recv_sem=leaf_recv.at[slot],
            device_id=where_is(peer),
            device_id_type=MESH,
        )

    def part_copy(peer, slot):
        return pltpu.make_async_remote_copy(
            src_ref=part_out.at[peer],
            dst_ref=part_in.at[mc],
            send_sem=part_send.at[peer],
            recv_sem=part_recv.at[slot],
            device_id=(mr, peer),
            device_id_type=MESH,
        )

    def pull_copy(peer, slot):
        return pltpu.make_async_remote_copy(
            src_ref=pull_out.at[peer],
            dst_ref=pulls.at[me],
            send_sem=pull_send.at[peer],
            recv_sem=pull_recv.at[slot],
            device_id=where_is(peer),
            device_id_type=MESH,
        )

    def each(size, here, act):
        def body(off, carry):
            act((here + off) % size)
            return carry

        lax.fori_loop(1, size, body, 0)

    each(cols, mc, lambda peer: act_copy(peer, mc).start())
    each(rows, mr, lambda peer: star_copy(peer, mr).start())
    each(count, me, lambda peer: list_copy(peer, me).start())
    lists_in[me] = lists[me]

    def prepare(r):
        table = star_all[r]
        row = row_of(table)
        body = (row != 3) & (row != 7)
        mass = table[3:4]
        right2[...] = stack_right(
            jnp.where(row < 3, -2.0 * table, jnp.where(row == 3, 1.0, 0.0)),
            sum3(table * table) + soft_star,
        )
        turned = swap(table)
        rightd[...] = stack_right(
            jnp.where(body, -turned, jnp.where(row == 7, 1.0, 0.0)), sum3(table * turned)
        )
        high, low = split2(jnp.where(body, table * mass, jnp.where(row == 3, mass, 0.0)))
        pad = jnp.zeros((weigh.shape[1] - 16, stars), F32)
        weigh[...] = jnp.concatenate([high, low, pad], 0).T.astype(BF16)

    def pairs(c):
        lhs = left[c]
        r2 = dot(lhs, right2[...])
        along = dot(lhs, rightd[...])
        inv = lax.rsqrt(r2)
        inv2 = inv * inv
        u = inv2 * inv
        q = u * inv2 * along
        uh, ul = cube_parts(u)
        qh, ql = cube_parts(q)
        w = weigh[...]
        acc_u[c] += dot(uh, w) + dot(ul, w)
        acc_q[c] += dot(qh, w) + dot(ql, w)

    def left_of(c):
        left[c] = stack_left(act_all[c]).T.astype(BF16)

    acc_u[...] = jnp.zeros_like(acc_u)
    acc_q[...] = jnp.zeros_like(acc_q)
    prepare(mr)
    left_of(mc)
    pairs(mc)

    def take_active(off, carry):
        c = (mc + off) % cols
        act_copy(c, c).wait_recv()
        left_of(c)
        pairs(c)
        return carry

    lax.fori_loop(1, cols, take_active, 0)

    each(count, me, lambda peer: list_copy(peer, peer).wait_recv())
    move = pltpu.make_async_copy(lists_in, lists_s, local_sem)
    move.start()
    move.wait()

    def grab(peer, ref):
        for s in range(slots):
            leaf = lists_s[peer, 0, s]
            live = leaf >= 0
            at = jnp.maximum(leaf, 0)
            keep = jnp.where(live, 1.0, 0.0)
            for c in range(3):
                ref[peer, 4 * s + c : 4 * s + c + 1, :] = gpos[c, pl.ds(at, 1), :] * keep
            ref[peer, 4 * s + 3 : 4 * s + 4, :] = gmass[pl.ds(at, 1), :] * keep
            keys[peer, 4 * s : 4 * s + 4, :] = jnp.full((4, width), leaf, jnp.int32)

    grab(me, leaves_in)

    def serve(peer):
        grab(peer, leaves_out)
        leaf_copy(peer, me).start()

    each(count, me, serve)

    key = keys[...].reshape(count * 4 * slots, width)
    component = row_of(key) % 4
    lane = lax.broadcasted_iota(jnp.int32, key.shape, 1)
    for c in range(3):
        match = jnp.where((key == lane) & (component == c), 1.0, 0.0)
        pick[c * width : (c + 1) * width, :] = match.T.astype(BF16)

    def take_stars(off, carry):
        r = (mr + off) % rows
        star_copy(r, r).wait_recv()
        prepare(r)

        def inner(c, carry):
            pairs(c)
            return carry

        lax.fori_loop(0, cols, inner, 0)
        return carry

    lax.fori_loop(1, rows, take_stars, 0)

    def finish(c):
        su = acc_u[c].T
        sq = acc_q[c].T
        su = su[0:8] + su[8:16]
        sq = sq[0:8] + sq[8:16]
        table = act_all[c]
        su = su - table * su[3:4]
        sq = sq - table * sq[3:4]
        return jnp.where(row8 < 4, su, su - 3.0 * swap(sq))

    def give(c):
        part_out[c] = finish(c)
        part_copy(c, mc).start()

    each(cols, mc, give)
    total = finish(mc)

    def collect(off, total):
        c = (mc + off) % cols
        part_copy(c, c).wait_recv()
        return total + part_in[c]

    total = lax.fori_loop(1, cols, collect, total)

    gap = (sel_b - total) * twelfth
    vel_one = sel_a + swap(sel_b + total) * (0.5 * step_length) + gap
    pos_one = sel_a + swap(sel_a + vel_one) * (0.5 * step_length) + gap
    new = jnp.where(row8 < 4, pos_one, vel_one)
    new = jnp.where(row8 == 3, 1.0, jnp.where(row8 == 7, 0.0, new))
    parts = jnp.concatenate(split3(new) + (jnp.zeros_like(new),), 0).astype(BF16)
    spread = dot_t(parts, onehot[...])
    spread = spread[0:8] + spread[8:16] + spread[16:24]
    fresh[...] = jnp.where(spread[3:4] > 0.5, spread, base_a[...])

    for b in range(nblock):
        at = pl.ds(b * width, width)
        table = fresh[:, at]
        mass = smass[b : b + 1, :]
        out_pos[:, b, :] = table[0:3]
        only = jnp.where(row8 < 3, table, 0.0)
        only = jnp.where(row8 == 3, sum3(only * only), only)
        sleft[b] = stack_left(only).T.astype(BF16)
        high, low = split2(jnp.where(row8 < 3, table * mass, jnp.where(row8 == 3, mass, 0.0)))
        both = jnp.concatenate([high, low], 0).astype(BF16)
        sfeat[b] = jnp.concatenate([both, both], 1)

    def entries(peer, ref):
        weights = []
        feats = []
        for s in range(slots):
            block = sblock[s, peer]
            at = jnp.maximum(block, 0)
            leaf = leaves_in[peer, 4 * s : 4 * s + 4, :]
            leaf = jnp.concatenate([leaf, jnp.zeros_like(leaf)], 0)
            row = row_of(leaf)
            mass = leaf[3:4]
            feat = stack_right(
                jnp.where(row < 3, -2.0 * leaf, jnp.where(row == 3, 1.0, 0.0)),
                sum3(leaf * leaf) + soft_galaxy,
            )
            inv = lax.rsqrt(dot(sleft[at], feat))
            uh, ul = cube_parts(inv * inv * inv)
            high, low = split2(jnp.where(row < 3, leaf * mass, jnp.where(row == 3, mass, 0.0)))
            both = jnp.concatenate([high, low], 0)
            both = jnp.concatenate(
                [both * jnp.where(block == b, 1.0, 0.0) for b in range(nblock)], 0
            ).astype(BF16)
            weights += [uh, ul]
            feats += [both, both]
            pull = dot(sfeat[at], jnp.concatenate([uh, ul], 0))
            pull = pull[0:8] + pull[8:16]
            pull = pull - leaf * pull[3:4]
            ref[peer, 4 * s : 4 * s + 4, :] = pull[0:4]
        kicks[...] += dot_t(jnp.concatenate(weights, 1), jnp.concatenate(feats, 1))

    def work(off, carry):
        peer = (me + off) % count
        leaf_copy(peer, peer).wait_recv()
        entries(peer, pull_out)
        pull_copy(peer, me).start()
        return carry

    kicks[...] = jnp.zeros_like(kicks)
    lax.fori_loop(1, count, work, 0)
    entries(me, pulls)
    turned = kicks[...].T
    for b in range(nblock):
        table = fresh[:, pl.ds(b * width, width)]
        kick = turned[16 * b : 16 * b + 8] + turned[16 * b + 8 : 16 * b + 16]
        kick = kick - table * kick[3:4]
        out_vel[:, b, :] = table[4:7] + step_length * kick[0:3]

    each(count, me, lambda peer: pull_copy(peer, peer).wait_recv())
    each(cols, mc, lambda peer: act_copy(peer, mc).wait_send())
    each(rows, mr, lambda peer: star_copy(peer, mr).wait_send())
    each(cols, mc, lambda peer: part_copy(peer, mc).wait_send())

    def drain(peer):
        list_copy(peer, me).wait_send()
        leaf_copy(peer, me).wait_send()
        pull_copy(peer, me).wait_send()

    each(count, me, drain)

    high, low = split2(pulls[...].reshape(count * 4 * slots, width))
    accel = dot(pick[...], high.astype(BF16)) + dot(pick[...], low.astype(BF16))
    accel = accel * float(nblock * count)
    for c in range(3):
        out_accel[c] = accel[c * width : (c + 1) * width]


def local(
    rows,
    cols,
    star_pos,
    star_vel,
    star_acc,
    star_jerk,
    star_mass,
    active_index,
    send_block,
    send_leaf,
    galaxy_pos,
    galaxy_mass,
):
    count = rows * cols
    nblock, _, width = star_pos.shape
    stars = nblock * width
    nact = active_index.shape[1]
    slots = send_leaf.shape[2]
    leaves, _, depth = galaxy_pos.shape
    lists = jnp.pad(send_leaf[0][:, None, :], ((0, 0), (0, 0), (0, 128 - slots)))
    vmem = pl.BlockSpec(memory_space=pltpu.VMEM)
    smem = pl.BlockSpec(memory_space=pltpu.SMEM)
    dma = pltpu.SemaphoreType.DMA
    pos, vel, accel = pl.pallas_call(
        functools.partial(kernel, rows, cols),
        out_shape=(
            jax.ShapeDtypeStruct((3, nblock, width), F32),
            jax.ShapeDtypeStruct((3, nblock, width), F32),
            jax.ShapeDtypeStruct((3, leaves, depth), F32),
        ),
        in_specs=[vmem] * 6 + [smem] + [vmem] * 3,
        out_specs=(vmem,) * 3,
        scratch_shapes=[
            pltpu.VMEM((8, stars), F32),
            pltpu.VMEM((8, stars), F32),
            pltpu.VMEM((stars, nact), BF16),
            pltpu.VMEM((cols, 8, nact), F32),
            pltpu.VMEM((rows, 8, stars), F32),
            pltpu.VMEM((cols, nact, 64), BF16),
            pltpu.VMEM((64, stars), BF16),
            pltpu.VMEM((64, stars), BF16),
            pltpu.VMEM((stars, 128), BF16),
            pltpu.VMEM((cols, nact, 128), F32),
            pltpu.VMEM((cols, nact, 128), F32),
            pltpu.VMEM((cols, 8, nact), F32),
            pltpu.VMEM((cols, 8, nact), F32),
            pltpu.VMEM((count, 4 * slots, depth), F32),
            pltpu.VMEM((count, 4 * slots, depth), F32),
            pltpu.VMEM((count, 4 * slots, depth), F32),
            pltpu.VMEM((count, 4 * slots, depth), F32),
            pltpu.VMEM((count, 4 * slots, depth), jnp.int32),
            pltpu.VMEM((3 * leaves, count * 4 * slots), BF16),
            pltpu.VMEM((width, 16 * nblock), F32),
            pltpu.VMEM((nblock, width, 64), BF16),
            pltpu.VMEM((nblock, 16, 2 * width), BF16),
            pltpu.VMEM((8, stars), F32),
            pltpu.VMEM((count, 1, 128), jnp.int32),
            pltpu.SMEM((count, 1, 128), jnp.int32),
            dma((count,)),
            dma((count,)),
            dma((cols,)),
            dma((cols,)),
            dma((rows,)),
            dma((rows,)),
            dma((count,)),
            dma((count,)),
            dma((cols,)),
            dma((cols,)),
            dma((count,)),
            dma((count,)),
            dma(()),
        ],
        compiler_params=pltpu.CompilerParams(
            collective_id=0, has_side_effects=True, vmem_limit_bytes=48 * 1024 * 1024
        ),
    )(
        star_pos.transpose(1, 0, 2),
        star_vel.transpose(1, 0, 2),
        star_acc.transpose(1, 0, 2),
        star_jerk.transpose(1, 0, 2),
        star_mass,
        active_index,
        send_block[0].T,
        lists,
        galaxy_pos.transpose(1, 0, 2),
        galaxy_mass,
    )
    return tuple(x.transpose(1, 0, 2) for x in (pos, vel, accel))


def solution(mesh):
    rows = mesh.shape["row"]
    cols = mesh.shape["col"]
    three = P(("row", "col"), None, None)
    two = P(("row", "col"), None)
    return jax.shard_map(
        functools.partial(local, rows, cols),
        mesh=mesh,
        in_specs=(three, three, three, three, two, two, three, three, three, two),
        out_specs=(three, three, three),
        check_vma=False,
    )
```

```python
import functools

import jax
import jax.numpy as jnp
from jax import lax
from jax.experimental import pallas as pl
from jax.experimental.pallas import tpu as pltpu
from jax.sharding import PartitionSpec as P

MESH = pl.DeviceIdType.MESH
step_length = 1.0
half = 0.5 * step_length**2
sixth = step_length**3 / 6.0
twelfth = step_length**2 / 12.0
soft_star = 0.01
soft_galaxy = 0.04
F32 = jnp.float32
BF16 = jnp.bfloat16


def row_of(x):
    return lax.broadcasted_iota(jnp.int32, x.shape, 0)


def swap(x):
    return pltpu.roll(x, 4, 0)


def rounded(x):
    return x.astype(BF16).astype(F32)


def split3(x):
    high = rounded(x)
    rest = x - high
    mid = rounded(rest)
    return high, mid, rest - mid


def split2(x):
    high = rounded(x)
    return high, x - high


def predict(a, b):
    pos = a + step_length * swap(a) + half * b + sixth * swap(b)
    vel = a + step_length * swap(b) + half * b
    return jnp.where(row_of(a) < 4, pos, vel)


def stack_left(table):
    high, mid, low = split3(table)
    ones = jnp.where(row_of(table) < 3, 1.0, 0.0)
    return jnp.concatenate([high, high, high, mid, mid, low, ones, jnp.zeros_like(table)], 0)


def stack_right(table, const):
    high, mid, low = split3(table)
    ch, cm, cl = split3(const)
    row = row_of(table)
    last = jnp.where(row == 0, ch, jnp.where(row == 1, cm, jnp.where(row == 2, cl, 0.0)))
    return jnp.concatenate(
        [high, mid, low, high, mid, high, last, jnp.zeros_like(table)], 0
    ).astype(BF16)


def sum3(x):
    return jnp.sum(jnp.where(row_of(x) < 3, x, 0.0), 0, keepdims=True)


def dot(a, b):
    return lax.dot_general(a, b, (((1,), (0,)), ((), ())), preferred_element_type=F32)


def dot_t(a, b):
    return lax.dot_general(a, b, (((1,), (1,)), ((), ())), preferred_element_type=F32)


def cube_parts(x):
    high = x.astype(BF16)
    return high, (x - high.astype(F32)).astype(BF16)


def kernel(
    rows,
    cols,
    spos,
    svel,
    sacc,
    sjerk,
    smass,
    index,
    sblock,
    lists,
    gpos_hbm,
    gmass_hbm,
    out_pos,
    out_vel,
    out_accel,
    base_a,
    base_b,
    onehot,
    act_all,
    star_all,
    left,
    right2,
    rightd,
    weigh,
    acc_u,
    acc_q,
    part_out,
    part_in,
    leaves_out,
    leaves_in,
    pull_out,
    pulls,
    keys,
    pick,
    kicks,
    sleft,
    sfeat,
    fresh,
    lists_in,
    lists_s,
    list_send,
    list_recv,
    act_send,
    act_recv,
    star_send,
    star_recv,
    leaf_send,
    leaf_recv,
    part_send,
    part_recv,
    pull_send,
    pull_recv,
    local_sem,
    all_here,
    gpos,
    gmass,
):
    mr = lax.axis_index("row")
    mc = lax.axis_index("col")
    count = rows * cols
    me = mr * cols + mc
    _, nblock, width = spos.shape
    slots = sblock.shape[0]
    stars = nblock * width
    nact = index.shape[1]

    def where_is(flat):
        return (flat // cols, flat % cols)

    barrier = pltpu.get_barrier_semaphore()

    def greet_col(off, carry):
        pl.semaphore_signal(
            barrier, inc=1, device_id=(mr, (mc + off) % cols), device_id_type=MESH
        )
        return carry

    def greet_row(off, carry):
        pl.semaphore_signal(
            barrier, inc=1, device_id=((mr + off) % rows, mc), device_id_type=MESH
        )
        return carry

    def vouch(off, carry):
        pl.semaphore_signal(
            all_here, inc=1, device_id=((mr + off) % rows, mc), device_id_type=MESH
        )
        return carry

    lax.fori_loop(1, cols, greet_col, 0)
    lax.fori_loop(1, rows, greet_row, 0)
    fetch_pos = pltpu.make_async_copy(gpos_hbm, gpos, local_sem.at[1])
    fetch_mass = pltpu.make_async_copy(gmass_hbm, gmass, local_sem.at[2])
    fetch_pos.start()
    fetch_mass.start()

    base_a[...] = jnp.zeros_like(base_a)
    base_b[...] = jnp.zeros_like(base_b)
    for b in range(nblock):
        at = pl.ds(b * width, width)
        base_a[0:3, at] = spos[:, b, :]
        base_a[4:7, at] = svel[:, b, :]
        base_b[0:3, at] = sacc[:, b, :]
        base_b[4:7, at] = sjerk[:, b, :]
    ta = base_a[...]
    tb = base_b[...]
    pred = predict(ta, tb)
    base_a[...] = pred
    for b in range(nblock):
        at = pl.ds(b * width, width)
        base_a[3:4, at] = smass[b : b + 1, :]
    star_all[mr] = base_a[...]
    hot = lax.broadcasted_iota(jnp.int32, (stars, nact), 0) == index[...]
    onehot[...] = hot.astype(F32).astype(BF16)
    parts = jnp.concatenate(split3(ta) + split3(tb), 0).astype(BF16)
    got = dot(parts, onehot[...])
    sel_a = got[0:8] + got[8:16] + got[16:24]
    sel_b = got[24:32] + got[32:40] + got[40:48]
    mine = predict(sel_a, sel_b)
    row8 = row_of(mine)
    mine = jnp.where(
        row8 == 3, sum3(mine * mine), jnp.where(row8 == 7, sum3(mine * swap(mine)), mine)
    )
    act_all[mc] = mine

    pl.semaphore_wait(barrier, cols + rows - 2)
    lax.fori_loop(1, rows, vouch, 0)

    def act_copy(peer, slot):
        return pltpu.make_async_remote_copy(
            src_ref=act_all.at[mc],
            dst_ref=act_all.at[mc],
            send_sem=act_send.at[peer],
            recv_sem=act_recv.at[slot],
            device_id=(mr, peer),
            device_id_type=MESH,
        )

    def star_copy(peer, slot):
        return pltpu.make_async_remote_copy(
            src_ref=star_all.at[mr],
            dst_ref=star_all.at[mr],
            send_sem=star_send.at[peer],
            recv_sem=star_recv.at[slot],
            device_id=(peer, mc),
            device_id_type=MESH,
        )

    def list_copy(peer, slot):
        return pltpu.make_async_remote_copy(
            src_ref=lists.at[peer],
            dst_ref=lists_in.at[me],
            send_sem=list_send.at[peer],
            recv_sem=list_recv.at[slot],
            device_id=where_is(peer),
            device_id_type=MESH,
        )

    def leaf_copy(peer, slot):
        return pltpu.make_async_remote_copy(
            src_ref=leaves_out.at[peer],
            dst_ref=leaves_in.at[me],
            send_sem=leaf_send.at[peer],
            recv_sem=leaf_recv.at[slot],
            device_id=where_is(peer),
            device_id_type=MESH,
        )

    def part_copy(peer, slot):
        return pltpu.make_async_remote_copy(
            src_ref=part_out.at[peer],
            dst_ref=part_in.at[mc],
            send_sem=part_send.at[peer],
            recv_sem=part_recv.at[slot],
            device_id=(mr, peer),
            device_id_type=MESH,
        )

    def pull_copy(peer, slot):
        return pltpu.make_async_remote_copy(
            src_ref=pull_out.at[peer],
            dst_ref=pulls.at[me],
            send_sem=pull_send.at[peer],
            recv_sem=pull_recv.at[slot],
            device_id=where_is(peer),
            device_id_type=MESH,
        )

    def each(size, here, act):
        def body(off, carry):
            act((here + off) % size)
            return carry

        lax.fori_loop(1, size, body, 0)

    each(cols, mc, lambda peer: act_copy(peer, mc).start())
    each(rows, mr, lambda peer: star_copy(peer, mr).start())
    lists_in[me] = lists[me]

    def prepare(r):
        table = star_all[r]
        row = row_of(table)
        body = (row != 3) & (row != 7)
        mass = table[3:4]
        right2[...] = stack_right(
            jnp.where(row < 3, -2.0 * table, jnp.where(row == 3, 1.0, 0.0)),
            sum3(table * table) + soft_star,
        )
        turned = swap(table)
        rightd[...] = stack_right(
            jnp.where(body, -turned, jnp.where(row == 7, 1.0, 0.0)), sum3(table * turned)
        )
        high, low = split2(jnp.where(body, table * mass, jnp.where(row == 3, mass, 0.0)))
        pad = jnp.zeros((weigh.shape[1] - 16, stars), F32)
        weigh[...] = jnp.concatenate([high, low, pad], 0).T.astype(BF16)

    group = 2 if cols % 2 == 0 else 1

    def pairs(c):
        lhs = left[c]
        r2 = dot(lhs, right2[...])
        along = dot(lhs, rightd[...])
        inv = lax.rsqrt(r2)
        inv2 = inv * inv
        u = inv2 * inv
        q = u * inv2 * along
        uh, ul = cube_parts(u)
        qh, ql = cube_parts(q)
        w = weigh[...]
        acc_u[c] += dot(uh, w) + dot(ul, w)
        acc_q[c] += dot(qh, w) + dot(ql, w)

    def left_of(c):
        left[c] = stack_left(act_all[c]).T.astype(BF16)

    acc_u[...] = jnp.zeros_like(acc_u)
    acc_q[...] = jnp.zeros_like(acc_q)
    prepare(mr)
    left_of(mc)
    pl.semaphore_wait(all_here, rows - 1)
    each(count, me, lambda peer: list_copy(peer, me).start())
    pairs(mc)

    def take_active(off, carry):
        c = (mc + off) % cols
        act_copy(c, c).wait_recv()
        left_of(c)
        pairs(c)
        return carry

    lax.fori_loop(1, cols, take_active, 0)

    each(count, me, lambda peer: list_copy(peer, peer).wait_recv())
    move = pltpu.make_async_copy(lists_in, lists_s, local_sem.at[0])
    fetch_pos.wait()
    fetch_mass.wait()
    move.start()
    move.wait()

    def grab(peer, ref):
        for s in range(slots):
            leaf = lists_s[peer, 0, s]
            live = leaf >= 0
            at = jnp.maximum(leaf, 0)
            keep = jnp.where(live, 1.0, 0.0)
            for c in range(3):
                ref[peer, 4 * s + c : 4 * s + c + 1, :] = gpos[c, pl.ds(at, 1), :] * keep
            ref[peer, 4 * s + 3 : 4 * s + 4, :] = gmass[pl.ds(at, 1), :] * keep
            keys[peer, 4 * s : 4 * s + 4, :] = jnp.full((4, width), leaf, jnp.int32)

    grab(me, leaves_in)

    def serve(peer):
        grab(peer, leaves_out)
        leaf_copy(peer, me).start()

    each(count, me, serve)

    key = keys[...].reshape(count * 4 * slots, width)
    component = row_of(key) % 4
    lane = lax.broadcasted_iota(jnp.int32, key.shape, 1)
    for c in range(3):
        match = jnp.where((key == lane) & (component == c), 1.0, 0.0)
        pick[c * width : (c + 1) * width, :] = match.T.astype(BF16)

    def take_stars(off, carry):
        r = (mr + off) % rows
        star_copy(r, r).wait_recv()
        prepare(r)

        def inner(c, carry):
            for k in range(group):
                pairs(c * group + k)
            return carry

        lax.fori_loop(0, cols // group, inner, 0)
        return carry

    lax.fori_loop(1, rows, take_stars, 0)

    def finish(c):
        su = acc_u[c].T
        sq = acc_q[c].T
        su = su[0:8] + su[8:16]
        sq = sq[0:8] + sq[8:16]
        table = act_all[c]
        su = su - table * su[3:4]
        sq = sq - table * sq[3:4]
        return jnp.where(row8 < 4, su, su - 3.0 * swap(sq))

    def give(c):
        part_out[c] = finish(c)
        part_copy(c, mc).start()

    each(cols, mc, give)
    total = finish(mc)

    def collect(off, total):
        c = (mc + off) % cols
        part_copy(c, c).wait_recv()
        return total + part_in[c]

    total = lax.fori_loop(1, cols, collect, total)

    gap = (sel_b - total) * twelfth
    vel_one = sel_a + swap(sel_b + total) * (0.5 * step_length) + gap
    pos_one = sel_a + swap(sel_a + vel_one) * (0.5 * step_length) + gap
    new = jnp.where(row8 < 4, pos_one, vel_one)
    new = jnp.where(row8 == 3, 1.0, jnp.where(row8 == 7, 0.0, new))
    parts = jnp.concatenate(split3(new) + (jnp.zeros_like(new),), 0).astype(BF16)
    spread = dot_t(parts, onehot[...])
    spread = spread[0:8] + spread[8:16] + spread[16:24]
    fresh[...] = jnp.where(spread[3:4] > 0.5, spread, base_a[...])

    for b in range(nblock):
        at = pl.ds(b * width, width)
        table = fresh[:, at]
        mass = smass[b : b + 1, :]
        out_pos[:, b, :] = table[0:3]
        only = jnp.where(row8 < 3, table, 0.0)
        only = jnp.where(row8 == 3, sum3(only * only), only)
        sleft[b] = stack_left(only).T.astype(BF16)
        high, low = split2(jnp.where(row8 < 3, table * mass, jnp.where(row8 == 3, mass, 0.0)))
        both = jnp.concatenate([high, low], 0).astype(BF16)
        sfeat[b] = jnp.concatenate([both, both], 1)

    def entries(work_list):
        weights = []
        feats = []
        for peer, ref, s in [(p, q, s) for p, q in work_list for s in range(slots)]:
            block = sblock[s, peer]
            at = jnp.maximum(block, 0)
            leaf = leaves_in[peer, 4 * s : 4 * s + 4, :]
            leaf = jnp.concatenate([leaf, jnp.zeros_like(leaf)], 0)
            row = row_of(leaf)
            mass = leaf[3:4]
            feat = stack_right(
                jnp.where(row < 3, -2.0 * leaf, jnp.where(row == 3, 1.0, 0.0)),
                sum3(leaf * leaf) + soft_galaxy,
            )
            inv = lax.rsqrt(dot(sleft[at], feat))
            uh, ul = cube_parts(inv * inv * inv)
            high, low = split2(jnp.where(row < 3, leaf * mass, jnp.where(row == 3, mass, 0.0)))
            both = jnp.concatenate([high, low], 0)
            both = jnp.concatenate(
                [both * jnp.where(block == b, 1.0, 0.0) for b in range(nblock)], 0
            ).astype(BF16)
            weights += [uh, ul]
            feats += [both, both]
            pull = dot(sfeat[at], jnp.concatenate([uh, ul], 0))
            pull = pull[0:8] + pull[8:16]
            pull = pull - leaf * pull[3:4]
            ref[peer, 4 * s : 4 * s + 4, :] = pull[0:4]
        kicks[...] += dot_t(jnp.concatenate(weights, 1), jnp.concatenate(feats, 1))

    def work(step, carry):
        peers = [(me + 2 * step + k) % count for k in (1, 2)]
        for peer in peers:
            leaf_copy(peer, peer).wait_recv()
        entries([(peer, pull_out) for peer in peers])
        for peer in peers:
            pull_copy(peer, me).start()
        return carry

    kicks[...] = jnp.zeros_like(kicks)
    lax.fori_loop(0, (count - 1) // 2, work, 0)
    rest = [(me + off) % count for off in range(1 + 2 * ((count - 1) // 2), count)]
    for peer in rest:
        leaf_copy(peer, peer).wait_recv()
    entries([(peer, pull_out) for peer in rest] + [(me, pulls)])
    for peer in rest:
        pull_copy(peer, me).start()
    turned = kicks[...].T
    for b in range(nblock):
        table = fresh[:, pl.ds(b * width, width)]
        kick = turned[16 * b : 16 * b + 8] + turned[16 * b + 8 : 16 * b + 16]
        kick = kick - table * kick[3:4]
        out_vel[:, b, :] = table[4:7] + step_length * kick[0:3]

    each(count, me, lambda peer: pull_copy(peer, peer).wait_recv())
    each(cols, mc, lambda peer: act_copy(peer, mc).wait_send())
    each(rows, mr, lambda peer: star_copy(peer, mr).wait_send())
    each(cols, mc, lambda peer: part_copy(peer, mc).wait_send())

    def drain(peer):
        list_copy(peer, me).wait_send()
        leaf_copy(peer, me).wait_send()
        pull_copy(peer, me).wait_send()

    each(count, me, drain)

    high, low = split2(pulls[...].reshape(count * 4 * slots, width))
    accel = dot(pick[...], high.astype(BF16)) + dot(pick[...], low.astype(BF16))
    accel = accel * float(nblock * count)
    for c in range(3):
        out_accel[c] = accel[c * width : (c + 1) * width]


def local(
    rows,
    cols,
    star_pos,
    star_vel,
    star_acc,
    star_jerk,
    star_mass,
    active_index,
    send_block,
    send_leaf,
    galaxy_pos,
    galaxy_mass,
):
    count = rows * cols
    nblock, _, width = star_pos.shape
    stars = nblock * width
    nact = active_index.shape[1]
    slots = send_leaf.shape[2]
    leaves, _, depth = galaxy_pos.shape
    lists = jnp.pad(send_leaf[0][:, None, :], ((0, 0), (0, 0), (0, 128 - slots)))
    vmem = pl.BlockSpec(memory_space=pltpu.VMEM)
    smem = pl.BlockSpec(memory_space=pltpu.SMEM)
    hbm = pl.BlockSpec(memory_space=pltpu.HBM)
    dma = pltpu.SemaphoreType.DMA
    pos, vel, accel = pl.pallas_call(
        functools.partial(kernel, rows, cols),
        out_shape=(
            jax.ShapeDtypeStruct((3, nblock, width), F32),
            jax.ShapeDtypeStruct((3, nblock, width), F32),
            jax.ShapeDtypeStruct((3, leaves, depth), F32),
        ),
        in_specs=[vmem] * 6 + [smem, vmem, hbm, hbm],
        out_specs=(vmem,) * 3,
        scratch_shapes=[
            pltpu.VMEM((8, stars), F32),
            pltpu.VMEM((8, stars), F32),
            pltpu.VMEM((stars, nact), BF16),
            pltpu.VMEM((cols, 8, nact), F32),
            pltpu.VMEM((rows, 8, stars), F32),
            pltpu.VMEM((cols, nact, 64), BF16),
            pltpu.VMEM((64, stars), BF16),
            pltpu.VMEM((64, stars), BF16),
            pltpu.VMEM((stars, 128), BF16),
            pltpu.VMEM((cols, nact, 128), F32),
            pltpu.VMEM((cols, nact, 128), F32),
            pltpu.VMEM((cols, 8, nact), F32),
            pltpu.VMEM((cols, 8, nact), F32),
            pltpu.VMEM((count, 4 * slots, depth), F32),
            pltpu.VMEM((count, 4 * slots, depth), F32),
            pltpu.VMEM((count, 4 * slots, depth), F32),
            pltpu.VMEM((count, 4 * slots, depth), F32),
            pltpu.VMEM((count, 4 * slots, depth), jnp.int32),
            pltpu.VMEM((3 * leaves, count * 4 * slots), BF16),
            pltpu.VMEM((width, 16 * nblock), F32),
            pltpu.VMEM((nblock, width, 64), BF16),
            pltpu.VMEM((nblock, 16, 2 * width), BF16),
            pltpu.VMEM((8, stars), F32),
            pltpu.VMEM((count, 1, 128), jnp.int32),
            pltpu.SMEM((count, 1, 128), jnp.int32),
            dma((count,)),
            dma((count,)),
            dma((cols,)),
            dma((cols,)),
            dma((rows,)),
            dma((rows,)),
            dma((count,)),
            dma((count,)),
            dma((cols,)),
            dma((cols,)),
            dma((count,)),
            dma((count,)),
            dma((3,)),
            pltpu.SemaphoreType.REGULAR,
            pltpu.VMEM((3, leaves, depth), F32),
            pltpu.VMEM((leaves, depth), F32),
        ],
        compiler_params=pltpu.CompilerParams(
            collective_id=0, has_side_effects=True, vmem_limit_bytes=48 * 1024 * 1024
        ),
    )(
        star_pos.transpose(1, 0, 2),
        star_vel.transpose(1, 0, 2),
        star_acc.transpose(1, 0, 2),
        star_jerk.transpose(1, 0, 2),
        star_mass,
        active_index,
        send_block[0].T,
        lists,
        galaxy_pos.transpose(1, 0, 2),
        galaxy_mass,
    )
    return tuple(x.transpose(1, 0, 2) for x in (pos, vel, accel))


def solution(mesh):
    rows = mesh.shape["row"]
    cols = mesh.shape["col"]
    three = P(("row", "col"), None, None)
    two = P(("row", "col"), None)
    return jax.shard_map(
        functools.partial(local, rows, cols),
        mesh=mesh,
        in_specs=(three, three, three, three, two, two, three, three, three, two),
        out_specs=(three, three, three),
        check_vma=False,
    )
```
